256 devices in a mesh: dp: 2 (over core), expert: 16 (over x, z_lo), tensor: 8 (over y, z_hi).
Axes of the slice: x: 4, y: 4, z: 8 (z_hi: 2, z_lo: 4; z = z_hi * 4 + z_lo), core: 2. Of those that a mesh axis runs over, the one named last changes fastest.
Arguments:
- tokens: bfloat16 [4096, 7168], P(('dp', 'expert'), 'tensor'), may hold values from -6 to 6
- cotangent: bfloat16 [4096, 7168], P(('dp', 'expert'), 'tensor'), may hold values from -6 to 6
- expert_ids: int32 [4096, 2], P(('dp', 'expert')), may hold values from 0 to 31, all different within a row; in each aligned block of 128 rows (0 to 127, 128 to 255, ...) at most 12 rows name the same one
- gate_values: float32 [4096, 2], P(('dp', 'expert')), may hold values from 0.1 to 0.9
- dense_up: bfloat16 [7168, 2432], P(('dp', 'expert'), 'tensor'), may hold values from -0.0625 to 0.0625
- dense_down: bfloat16 [2432, 7168], P('tensor', ('dp', 'expert')), may hold values from -0.125 to 0.125
- expert_up: bfloat16 [32, 7168, 2432], P(('dp', 'expert'), 'tensor'), may hold values from -0.0625 to 0.0625
- expert_down: bfloat16 [32, 2432, 7168], P(('dp', 'expert'), None, 'tensor'), may hold values from -0.125 to 0.125
Outputs:
- input_grad: bfloat16 [4096, 7168], P(('dp', 'expert'), 'tensor')
- dense_up_grad: bfloat16 [7168, 2432], P(('dp', 'expert'), 'tensor')
- dense_down_grad: bfloat16 [2432, 7168], P('tensor', ('dp', 'expert'))
The draws below stay inside these ranges and needn't reach their ends.
Inputs may be any that keep to these rules, and one draw needn't show every extreme that they name: `expert_ids`: each token names two different experts. Among the 128 tokens of one index of dp and expert (aligned blocks of rows), no expert is named more than 12 times, a bound that some block reaches in every draw.
All inputs are finite; a program needn't handle non-finite values.
Results may differ from the reference program's by a relative error of at most 0.005.
Values may be sent and summed in bfloat16 or wider, within the bound.
No kernel may reach another device: no remote copies, remote signals or barrier semaphores. Data moves between devices by JAX's collectives and lax.ppermute only.
A program may use at most 192 MiB of HBM per device.

```python
import math
import jax
import jax.numpy as jnp
import numpy as np
from jax import lax

D = 7168
FFD = 2432
FFE = 2432
TOK_DEV = 128
EXPERTS = 32
TOKENS = 4096
CAP = 12
N_DP = 2
N_EXPERT = 16


def with_spikes(entries, stream_key, source, target, parts, factor):
    def block_of(dim):
        return (jnp.arange(entries.shape[dim]) // (entries.shape[dim] // parts)).reshape((-1,) + (1,) * (entries.ndim - 1 - dim))

    near = jax.random.permutation(stream_key, parts)[block_of(target)]
    far = (block_of(target) + parts // 2) % parts
    return jnp.where((block_of(source) == near) | (block_of(source) == far), factor * entries, entries)


def shard_levels(key, extent, shards, low, high):
    gain, own = 1.0, jax.random.fold_in(key, 6)
    for dim, blocks in shards:
        heights = jnp.exp(jax.random.uniform(jax.random.fold_in(own, dim), (blocks,), jnp.float32, low / len(shards), high / len(shards)))
        gain = gain * jnp.repeat(heights, extent[dim] // blocks).reshape([-1 if axis == dim else 1 for axis in range(len(extent))])
    return gain


def routed_block(key, own, number, rows, number_of, top, most, slope):
    order = jax.random.permutation(key, number_of)
    heavy_load, usual = shares(number_of, rows * top, most, slope, True), shares(number_of, rows * top, most, slope, False)
    places = jnp.arange(number_of)

    def named(tallies, rotation):
        used = int((tallies > 0).sum())
        fixed = max(1, used // 4)
        moved = fixed + (places - fixed + rotation * (used - fixed)) % max(1, number_of - fixed)
        return jnp.zeros((number_of,), jnp.int32).at[order[jnp.where(places < fixed, places, moved)]].set(jnp.asarray(tallies, jnp.int32))

    tallies = jnp.where(number % 4 == 0, named(heavy_load, number // 4), named(usual, number - number // 4 - 1))
    mixed = jax.random.permutation(jax.random.fold_in(own, 3), number_of)
    source_of, receiver = mixed[0:number_of // 2 * 2:2], mixed[1:number_of // 2 * 2:2]
    room = jnp.minimum(tallies[source_of] - 1, most - tallies[receiver]) // 2
    room = jnp.where((source_of == order[0]) | (receiver == order[0]) | (tallies[receiver] == 0), 0, jnp.maximum(room, 0))
    moved = jax.random.randint(jax.random.fold_in(own, 4), (number_of // 2,), 0, 1 << 20) % (room + 1)
    tallies = tallies.at[source_of].add(-moved).at[receiver].add(moved)
    items = jnp.searchsorted(jnp.cumsum(tallies), jnp.arange(rows * top), side="right").astype(jnp.int32)
    table = items.reshape(top, rows).T
    table = table[jax.random.permutation(jax.random.fold_in(own, 1), rows)]
    rotation = jax.random.randint(jax.random.fold_in(own, 2), (rows, 1), 0, top)
    return jnp.take_along_axis(table, (jnp.arange(top)[None, :] + rotation) % top, axis=1)


def shares(amount, total, reach, skew, full):
    loads = [(1 << 20) // math.isqrt(rank ** skew) + 1 for rank in range(1, amount + 1)]
    largest = reach if full else min(reach, max(-(-total // amount), total * loads[0] // sum(loads)))
    least = 1 if total - largest >= amount - 1 else 0
    holding, rest = [largest] + [least] * (amount - 1), total - largest - least * (amount - 1)
    while rest > 0:
        free = [i for i in range(1, amount) if holding[i] < largest] or [i for i in range(1, amount) if holding[i] < reach]
        pool, remaining = sum([loads[i] for i in free]), rest
        for i in free:
            extra = min(reach - holding[i], max(1, remaining * loads[i] // pool), rest)
            holding[i] = holding[i] + extra
            rest = rest - extra
    return np.array(holding)


def gaussian(rng, extent, width, most, cuts=(), kind=jnp.bfloat16):
    gain = shard_levels(rng, extent, cuts, -0.22, 0.18) if cuts else 1.0
    drawn = jax.random.normal(rng, extent, jnp.float32) * width * gain
    return jnp.minimum(jnp.maximum(drawn, -most), most).astype(kind)


def gaussian_with(rng, extent, scale, bound, split, heavy, held_as=jnp.bfloat16):
    result = scale * jax.random.normal(rng, extent, jnp.float32)
    if split:
        result = result * shard_levels(rng, extent, split, -0.22, 0.18)
    return jnp.clip(with_spikes(result, jax.random.fold_in(rng, 3), *heavy), -bound, bound).astype(held_as)


def setup_inputs(seed: int = 0) -> dict:
    keys = jax.random.split(jax.random.key(seed), 9)
    tokens = gaussian_with(keys[0], (TOKENS, D), 1.0, 6.0, ((0, 32), (1, 8)), (0, 1, 32, 2.75))
    cotangent = gaussian_with(keys[1], (TOKENS, D), 1.0, 6.0, ((0, 32), (1, 8)), (0, 1, 32, 2.75))
    expert_ids_keys = jax.random.split(jax.random.fold_in(keys[2], 1), TOKENS // TOK_DEV)
    expert_ids_turns = jax.random.permutation(jax.random.fold_in(keys[2], 3), TOKENS // TOK_DEV)
    expert_ids = jax.vmap(lambda own, number: routed_block(jax.random.fold_in(keys[2], 2), own, number, TOK_DEV, EXPERTS, 2, CAP, 2))(expert_ids_keys, expert_ids_turns).reshape((TOKENS, 2))
    gate_values = jnp.clip(0.1 + 0.79999997 * jax.random.uniform(keys[3], (TOKENS, 2), jnp.float32) ** shard_levels(keys[3], (TOKENS, 2), ((0, 32),), -0.2, 0.2), 0.1, 0.9)
    dense_up = gaussian(keys[4], (D, FFD), D ** -0.5, 0.0625, ((0, 32), (1, 8)))
    dense_down = gaussian(keys[5], (FFD, D), FFD ** -0.5, 0.125, ((0, 8), (1, 32)))
    expert_up = gaussian(keys[6], (EXPERTS, D, FFE), D ** -0.5, 0.0625, ((0, 32), (1, 8)))
    expert_down = gaussian(keys[7], (EXPERTS, FFE, D), FFE ** -0.5, 0.125, ((0, 32), (2, 8)))
    return dict(tokens=tokens, cotangent=cotangent, expert_ids=expert_ids, gate_values=gate_values, dense_up=dense_up, dense_down=dense_down, expert_up=expert_up, expert_down=expert_down)


def silu_slope(values):
    sigma = jax.nn.sigmoid(values)
    return sigma * (1.0 + values * (1.0 - sigma))

def rounded(values):
    return lax.optimization_barrier(values.astype(jnp.bfloat16)).astype(jnp.float32)

def reference(tokens, cotangent, expert_ids, gate_values, dense_up, dense_down, expert_up, expert_down):
    grad_scale = 1.0 / math.sqrt(TOKENS)
    contract_last = (((1,), (1,)), ((), ()))
    contract_first = (((0,), (0,)), ((), ()))
    dense_pre = jnp.dot(tokens, dense_up, preferred_element_type=jnp.float32)
    dense_hidden = jax.nn.silu(dense_pre).astype(jnp.bfloat16)
    dense_dhid = lax.dot_general(cotangent, dense_down, contract_last, preferred_element_type=jnp.float32)
    dense_dpre = (dense_dhid * silu_slope(dense_pre)).astype(jnp.bfloat16)
    dense_input_grad = lax.dot_general(dense_dpre, dense_up, contract_last, preferred_element_type=jnp.float32)
    up_total = lax.dot_general(tokens, dense_dpre, contract_first, preferred_element_type=jnp.float32) * grad_scale
    down_total = lax.dot_general(dense_hidden, cotangent, contract_first, preferred_element_type=jnp.float32) * grad_scale
    max_rows = N_DP * N_EXPERT * CAP
    flat_ids = expert_ids.reshape(-1)
    flat_gates = gate_values.reshape(-1)

    def one_expert(accumulated, inputs):
        up_slab, down_slab, expert_num = inputs
        chosen = flat_ids == expert_num
        live_count = jnp.sum(chosen.astype(jnp.int32))
        pick_index = jnp.nonzero(chosen, size=max_rows, fill_value=0)[0].astype(jnp.int32)
        live_mask = jnp.arange(max_rows, dtype=jnp.int32) < live_count
        token_rows = (pick_index // 2).astype(jnp.int32)
        rows_x = tokens[token_rows]
        rows_dy = cotangent[token_rows]
        expert_pre = jnp.dot(rows_x, up_slab, preferred_element_type=jnp.float32)
        expert_dhid = lax.dot_general(rows_dy, down_slab, contract_last, preferred_element_type=jnp.float32)
        expert_dpre = (expert_dhid * silu_slope(expert_pre)).astype(jnp.bfloat16)
        expert_back = lax.dot_general(expert_dpre, up_slab, contract_last, preferred_element_type=jnp.float32)
        weights_used = jnp.where(live_mask, flat_gates[pick_index], jnp.float32(0.0))
        contribution = rounded(expert_back) * weights_used[:, None]
        return (accumulated.at[token_rows].add(contribution), None)
    expert_total, _ = lax.scan(one_expert, jnp.zeros((TOKENS, D), jnp.float32), (expert_up, expert_down, jnp.arange(EXPERTS, dtype=jnp.int32)))
    input_grad = (cotangent.astype(jnp.float32) + dense_input_grad + expert_total).astype(jnp.bfloat16)
    return (input_grad, up_total.astype(jnp.bfloat16), down_total.astype(jnp.bfloat16))
```

```python
import math

import jax
import jax.numpy as jnp
import numpy as np
from jax import lax
from jax.sharding import Mesh, PartitionSpec as P

AXES = ("dp", "x", "zl", "y", "zh")
SIZES = (2, 4, 4, 4, 2)
BF16 = jnp.bfloat16
F32 = jnp.float32
CAP = 12
WIDTH = 304


def weight_moves():
    moves = []
    for source in range(256):
        dp, x, zl, y, zh = np.unravel_index(source, SIZES)
        feature_block, hidden_block = dp * 4 + x, y * 2 + zh
        target = np.ravel_multi_index(
            (hidden_block // 4, hidden_block % 4, zl, feature_block // 2, feature_block % 2), SIZES
        )
        moves.append((source, int(target)))
    return moves


def silu_slope(values):
    sigma = jax.nn.sigmoid(values)
    return sigma * (1.0 + values * (1.0 - sigma))


def send(values, axis, size, step):
    return lax.ppermute(values, axis, [(i, (i + step) % size) for i in range(size)])


def dot(a, b, ca, cb):
    return lax.dot_general(a, b, (((ca,), (cb,)), ((), ())), preferred_element_type=F32)


def local(tokens, cotangent, expert_ids, gate_values, dense_up, dense_down, expert_up, expert_down):
    rows = tokens.shape[0]
    width = tokens.shape[1]
    my_dp = lax.axis_index("dp")
    my_y = lax.axis_index("y")
    my_zh = lax.axis_index("zh")
    my_zl = lax.axis_index("zl")
    grad_scale = 1.0 / math.sqrt(rows * 32)
    up = expert_up[0]
    down = expert_down[0]

    with jax.named_scope("route"):
        ids = expert_ids.T.reshape(-1)
        hot = (ids[:, None] == jnp.arange(32, dtype=jnp.int32)[None, :]).astype(F32)
        order = jnp.arange(2 * rows)
        lower = (order[:, None] > order[None, :]).astype(F32)
        before = dot(lower, hot, 1, 0)
        position = jnp.sum(before * hot, axis=1).astype(jnp.int32)
        place = (ids % 16) * 2 + ids // 16
        row_of = (place * 24 + position).reshape(2, rows)
        pair = jnp.concatenate([tokens, cotangent], axis=0)
        out_row = jnp.arange(768, dtype=jnp.int32)
        is_cot = (out_row % 24) >= CAP
        wanted = jnp.where(is_cot, out_row - CAP, out_row)
        col_cot = jnp.arange(2 * rows) >= rows
        row_two = jnp.concatenate([row_of, row_of], axis=1)
        select = (wanted[:, None] == row_two[0][None, :]) | (wanted[:, None] == row_two[1][None, :])
        select = select & (is_cot[:, None] == col_cot[None, :])
        packed = dot(select.astype(BF16), pair, 1, 0).astype(BF16)
    with jax.named_scope("to_experts"):
        arrived = lax.all_to_all(
            packed.reshape(32, 24, width), ("x", "zl", "dp"), split_axis=0, concat_axis=0, tiled=True
        ).reshape(4, 192, width)

    with jax.named_scope("dense_weights"):
        weights = jnp.concatenate([dense_up, dense_down.T], axis=1)
        weights = lax.ppermute(weights, AXES, weight_moves())
        blocks = [weights] + [send(weights, "zl", 4, -k) for k in (1, 2, 3)]
        blocks = jnp.stack(blocks + blocks[:3])
        weights = lax.dynamic_slice_in_dim(blocks, (4 - my_zl) % 4, 4, 0).reshape(896, 2 * WIDTH)
        dense_u = weights[:, :WIDTH]
        dense_d = weights[:, WIDTH:]

    with jax.named_scope("dense_tokens"):
        gathered = jnp.stack([pair] + [send(pair, "x", 4, -k) for k in (1, 2, 3)])
        gathered = jnp.concatenate([gathered, send(gathered, "dp", 2, 1)], axis=0)
        gathered = gathered.reshape(4, 2, 2, rows, width)
        gathered = jnp.concatenate([gathered, gathered], axis=0)
        gathered = lax.dynamic_slice_in_dim(gathered, my_y, 4, 0)
        all_x = gathered[:, :, 0].reshape(4, 2 * rows, width)
        all_c = gathered[:, :, 1].reshape(4, 2 * rows, width)

    with jax.named_scope("expert_sums"):
        i192 = jnp.arange(192, dtype=jnp.int32)
        source_row = (i192 % 96) // CAP * 24 + (i192 % 96) % CAP + (i192 // 96) * CAP
        split = (source_row[:, None] == i192[None, :]).astype(BF16)
        own_sums = None
        received = []
        chunks = {}
        for k in (2, 1, 3, 0):
            chunk = lax.dynamic_index_in_dim(arrived, (my_y + k) % 4, 0, keepdims=False)
            chunks[k] = dot(split, chunk, 1, 0).astype(BF16)
        pre_sum = dot(chunks[0][:96], up, 1, 0)
        hid_sum = dot(chunks[0][96:], down, 1, 1)
        pre_in = [send(dot(chunks[k][:96], up, 1, 0).astype(BF16), "y", 4, k) for k in (2, 1, 3)]
        hid_in = [send(dot(chunks[k][96:], down, 1, 1).astype(BF16), "y", 4, k) for k in (2, 1, 3)]

        def over_zh(total, size, axis):
            mine = lax.dynamic_slice_in_dim(total, my_zh * size, size, axis)
            other = lax.dynamic_slice_in_dim(total, (1 - my_zh) * size, size, axis)
            return mine + send(other.astype(BF16), "zh", 2, 1).astype(F32)

        pre_sum = over_zh(pre_sum + sum(v.astype(F32) for v in pre_in), 48, 0)
        hid_sum = over_zh(hid_sum + sum(v.astype(F32) for v in hid_in), 48, 0)
        dpre = (hid_sum * silu_slope(pre_sum)).astype(BF16)

    def both_halves(mine, axis):
        other = send(mine, "zh", 2, 1)
        return jnp.where(
            my_zh == 0, jnp.concatenate([mine, other], axis), jnp.concatenate([other, mine], axis)
        )

    with jax.named_scope("expert_back"):
        dpre = both_halves(dpre, 0)
        parts = [dpre] + [send(dpre, "y", 4, -k) for k in (1, 2, 3)]
        back = [dot(v, up, 1, 1).astype(BF16) for v in parts]
        back = jnp.stack(back + back[:3])
        back = lax.dynamic_slice_in_dim(back, (4 - my_y) % 4, 4, 0).reshape(16, 24, width)
        returned = lax.all_to_all(back, ("x", "zl"), split_axis=0, concat_axis=0, tiled=True)
        returned = returned.reshape(384, width)

    with jax.named_scope("expert_combine"):
        info = jnp.concatenate([row_of.astype(F32), ids.reshape(2, rows).astype(F32), gate_values.T], axis=0)
        other_info = send(info, "dp", 2, 1)

        def combine(table, target_dp):
            total = jnp.zeros((rows, width), F32)
            for k in (0, 1):
                row = table[k].astype(jnp.int32)
                expert = table[2 + k].astype(jnp.int32)
                row = (expert % 16) * 24 + target_dp * CAP + (row % 24)
                row = jnp.where(expert // 16 == my_dp, row, -1)
                pick = (row[:, None] == jnp.arange(384, dtype=jnp.int32)[None, :]).astype(BF16)
                total = total + dot(pick, returned, 1, 0) * table[4 + k][:, None]
            return total

        expert_input = combine(info, my_dp)
        other_input = combine(other_info, 1 - my_dp).astype(BF16)
        expert_input = expert_input + send(other_input, "dp", 2, 1).astype(F32)

    with jax.named_scope("dense_sums"):
        def dense_chunk(k):
            return jnp.concatenate([dot(dense_u, all_x[k], 0, 1), dot(dense_d, all_c[k], 0, 1)], axis=0)

        total = dense_chunk(0)
        arriving = [send(dense_chunk(k).astype(BF16), "y", 4, k) for k in (2, 1, 3)]
        total = over_zh(total + sum(v.astype(F32) for v in arriving), rows, 1)
        d_pre, d_hid = total[:WIDTH], total[WIDTH:]
        both = jnp.concatenate(
            [(d_hid * silu_slope(d_pre)).astype(BF16), jax.nn.silu(d_pre).astype(BF16)], axis=0
        )
        both = both_halves(both, 1)
        parts = [both] + [send(both, "y", 4, -k) for k in (1, 2, 3)]

    with jax.named_scope("dense_grads"):
        whole = jnp.concatenate(parts, axis=1)
        flat_x = all_x.reshape(8 * rows, width)
        flat_c = all_c.reshape(8 * rows, width)
        grad_u = dot(flat_x, whole[:WIDTH], 0, 1)
        grad_d = dot(flat_c, whole[WIDTH:], 0, 1)
        grads = jnp.concatenate([grad_u, grad_d], axis=1).reshape(4, 224, 2 * WIDTH) * grad_scale

        def grad_block(k):
            return lax.dynamic_index_in_dim(grads, (my_zl + k) % 4, 0, keepdims=False)

        total = grad_block(0)
        arriving = [send(grad_block(k).astype(BF16), "zl", 4, k) for k in (2, 1, 3)]
        total = (total + sum(v.astype(F32) for v in arriving)).astype(BF16)
        total = lax.ppermute(total, AXES, [(b, a) for a, b in weight_moves()])
        up_grad = total[:, :WIDTH]
        down_grad = total[:, WIDTH:].T

    with jax.named_scope("dense_input"):
        back = dot(whole[:WIDTH], dense_u, 0, 1).reshape(4, 2 * rows, width)
        back = jnp.concatenate([back, back], axis=0)
        back = lax.dynamic_slice_in_dim(back, (4 - my_y) % 4, 4, 0).reshape(2, 4, rows, width)
        mine = back[0] + send(back[1].astype(BF16), "dp", 2, 1).astype(F32)
        arriving = [send(mine[k].astype(BF16), "x", 4, k) for k in (2, 1, 3)]
        dense_input = mine[0] + sum(v.astype(F32) for v in arriving)

    input_grad = (cotangent.astype(F32) + dense_input + expert_input).astype(BF16)
    return (input_grad, up_grad, down_grad)


def solution(mesh):
    split = Mesh(mesh.devices.reshape(SIZES), AXES)
    group, tensor = ("dp", "x", "zl"), ("y", "zh")
    return jax.shard_map(
        local,
        mesh=split,
        in_specs=(
            P(group, tensor),
            P(group, tensor),
            P(group, None),
            P(group, None),
            P(group, tensor),
            P(tensor, group),
            P(group, tensor, None),
            P(group, None, tensor),
        ),
        out_specs=(
            P(group, tensor),
            P(group, tensor),
            P(tensor, group),
        ),
        check_vma=False,
    )
```

```python
import math

import jax
import jax.numpy as jnp
import numpy as np
from jax import lax
from jax.experimental import pallas as pl
from jax.experimental.pallas import tpu as pltpu
from jax.sharding import Mesh, PartitionSpec as P

AXES = ("dp", "x", "zl", "y", "zh")
SIZES = (2, 4, 4, 4, 2)
BF16 = jnp.bfloat16
F32 = jnp.float32
CAP = 12
WIDTH = 304


def weight_moves(flip=0):
    moves = []
    for source in range(256):
        dp, x, zl, y, zh = np.unravel_index(source, SIZES)
        feature_block, hidden_block = dp * 4 + x, y * 2 + zh
        target = np.ravel_multi_index(
            (hidden_block // 4, hidden_block % 4, zl ^ flip, feature_block // 2, feature_block % 2), SIZES
        )
        moves.append((source, int(target)))
    return moves


def silu_slope(values):
    sigma = jax.nn.sigmoid(values)
    return sigma * (1.0 + values * (1.0 - sigma))


def send(values, axis, size, step):
    return lax.ppermute(values, axis, [(i, (i + step) % size) for i in range(size)])


def dot(a, b, ca, cb):
    return lax.dot_general(a, b, (((ca,), (cb,)), ((), ())), preferred_element_type=F32)


def swap(values, axis, size, bit):
    return lax.ppermute(values, axis, [(i, i ^ bit) for i in range(size)])


def kernel(fn, outs, *arrays):
    def body(*refs):
        results = fn(*[r[...] for r in refs[: len(arrays)]])
        for ref, value in zip(refs[len(arrays) :], results, strict=True):
            ref[...] = value.astype(ref.dtype)

    vmem = pl.BlockSpec(memory_space=pltpu.VMEM)
    return pl.pallas_call(
        body,
        out_shape=[jax.ShapeDtypeStruct(shape, dtype) for shape, dtype in outs],
        in_specs=[vmem] * len(arrays),
        out_specs=[vmem] * len(outs),
        cost_estimate=pl.CostEstimate(flops=0, bytes_accessed=0, transcendentals=0),
        compiler_params=pltpu.CompilerParams(vmem_limit_bytes=40 * 1024 * 1024),
    )(*arrays)


def after(values, *earlier):
    return lax.optimization_barrier((values,) + earlier)[0]


def spread(chunks):
    return [send(chunks[k].astype(BF16), "y", 4, k) for k in (2, 1, 3)]


def add_up(own, arriving):
    return own + sum(v.astype(F32) for v in arriving)


def spread_gather(block, axis):
    return jnp.concatenate([block] + [send(block, "y", 4, -k) for k in (1, 2, 3)], axis=axis)


def local(tokens, cotangent, expert_ids, gate_values, dense_up, dense_down, expert_up, expert_down):
    rows = tokens.shape[0]
    width = tokens.shape[1]
    my_dp = lax.axis_index("dp")
    my_y = lax.axis_index("y")
    my_zh = lax.axis_index("zh")
    my_zl = lax.axis_index("zl")
    grad_scale = 1.0 / math.sqrt(rows * 32)
    up = expert_up[0]
    down = expert_down[0]

    with jax.named_scope("route"):
        ids = expert_ids.T.reshape(-1)
        hot = (ids[:, None] == jnp.arange(32, dtype=jnp.int32)[None, :]).astype(F32)
        order = jnp.arange(2 * rows)
        lower = (order[:, None] > order[None, :]).astype(F32)
        before = dot(lower, hot, 1, 0)
        position = jnp.sum(before * hot, axis=1).astype(jnp.int32)
        row_of = ((ids % 16) * 24 + (ids // 16) * CAP + position).reshape(2, rows)
        out_row = jnp.arange(384, dtype=jnp.int32)
        select = (out_row[:, None] == row_of[0][None, :]) | (out_row[:, None] == row_of[1][None, :])
        select = select.astype(BF16)
        packed_x = dot(select, tokens, 1, 0).astype(BF16).reshape(16, 24, width)
        packed_c = dot(select, cotangent, 1, 0).astype(BF16).reshape(16, 24, width)

    with jax.named_scope("to_experts"):
        r = jnp.arange(192, dtype=jnp.int32)
        theirs = (r // CAP) * 24 + (1 - my_dp) * CAP + r % CAP
        rolled = (out_row + my_y * 96) % 384
        block, core, slot = rolled // 24, (rolled // CAP) % 2, rolled % CAP
        from_got = jnp.where(core == my_dp, block * 24 + my_dp * CAP + slot, -1)
        from_other = jnp.where(core == my_dp, -1, block * CAP + slot)
        pick_theirs = (theirs[:, None] == out_row[None, :]).astype(BF16)
        pick_got = (from_got[:, None] == out_row[None, :]).astype(BF16)
        pick_other = (from_other[:, None] == r[None, :]).astype(BF16)

        def to_chip(packed):
            return lax.all_to_all(packed, ("x", "zl"), split_axis=0, concat_axis=0, tiled=True).reshape(384, width)

        def to_core(got):
            theirs = kernel(lambda p, g: [dot(p, g, 1, 0)], [((192, width), BF16)], pick_theirs, got)[0]
            other = send(theirs, "dp", 2, 1)
            return kernel(
                lambda p, g, q, o: [dot(p, g, 1, 0) + dot(q, o, 1, 0)],
                [((384, width), BF16)],
                pick_got, got, pick_other, other,
            )[0]

        got_x = to_chip(packed_x)
        weights = jnp.concatenate([dense_up, dense_down.T], axis=1)
        weights = lax.ppermute(weights, AXES, weight_moves())
        got_c = to_chip(after(packed_c, got_x))
        far = swap(weights, "zl", 4, 2)
        expert_x = to_core(got_x)

    def zh_parts(total, size, axis):
        mine = lax.dynamic_slice_in_dim(total, my_zh * size, size, axis)
        other = lax.dynamic_slice_in_dim(total, (1 - my_zh) * size, size, axis)
        return mine, send(other.astype(BF16), "zh", 2, 1)

    zh_here = jnp.full((8, 128), my_zh, jnp.int32)

    def sum_parts(own, arriving):
        half = (own.shape[0] // 2, own.shape[1])

        def body(own, a, b, c, here):
            total = own + a.astype(F32) + b.astype(F32) + c.astype(F32)
            low, high = total[: half[0]], total[half[0] :]
            first = here[0, 0] == 0
            return jnp.where(first, low, high), jnp.where(first, high, low)

        mine, other = kernel(body, [(half, F32), (half, BF16)], own, *arriving, zh_here)
        return mine, send(other, "zh", 2, 1)

    def both_halves(mine, other, axis):
        return jnp.where(
            my_zh == 0, jnp.concatenate([mine, other], axis), jnp.concatenate([other, mine], axis)
        )

    with jax.named_scope("expert_pre"):
        chunk = (96, up.shape[1])
        chunk_outs = [(chunk, F32)] + [(chunk, BF16)] * 3

        def products(weight_dim):
            def body(lines, weight):
                return [dot(lines[96 * k : 96 * k + 96], weight, 1, weight_dim) for k in range(4)]

            return body

        pre = dict(enumerate(kernel(products(0), chunk_outs, expert_x, up)))
        pre_in = spread(pre)

    with jax.named_scope("tokens_move"):
        gathered = lax.all_gather(jnp.concatenate([tokens, cotangent], axis=0), "x", axis=0)

    with jax.named_scope("expert_hid"):
        expert_c = to_core(after(got_c, weights, *pre.values()))
        hid = dict(enumerate(kernel(products(1), chunk_outs, expert_c, down)))
        hid_in = spread(hid)

    with jax.named_scope("expert_pre"):
        pre_in, gathered, far = after([pre_in, gathered, far], *hid.values())
        low = my_zl < 2
        two = jnp.stack([jnp.where(low, weights, far), jnp.where(low, far, weights)])
        near = swap(two, "zl", 4, 1)
        pre_mine, pre_other = sum_parts(pre[0], pre_in)

    with jax.named_scope("tokens_move"):
        crossed = send(gathered, "dp", 2, 1)

    with jax.named_scope("dense_sums"):
        def dense_body(y_ref, even_ref, own_ref, cross_ref, two_ref, near_ref, *outs):
            chunk_refs, xt_ref, ct_ref, w_ref = outs[:4], outs[4], outs[5], outs[6]
            even = even_ref[0] == 0
            for upper in range(2):
                a, b = two_ref[upper], near_ref[upper]
                w_ref[448 * upper : 448 * upper + 224, :] = jnp.where(even, a, b)
                w_ref[448 * upper + 224 : 448 * upper + 448, :] = jnp.where(even, b, a)
            is_pre = lax.broadcasted_iota(jnp.int32, (rows, 2 * WIDTH), 1) < WIDTH
            for k in range(4):
                block = lax.rem(y_ref[0] + k, 4)
                first = 2 * lax.rem(block, 2)
                w = w_ref[...]
                for i in range(2):
                    both = jnp.where(block < 2, own_ref[first + i], cross_ref[first + i])
                    lines = pl.ds(rows * i, rows)
                    lanes = pl.ds(2 * rows * k + rows * i, rows)
                    xt_ref[:, lanes] = both[:rows].T
                    ct_ref[:, lanes] = both[rows:].T
                    products = dot(both, w, 1, 0)
                    value = jnp.where(is_pre, products[:rows], products[rows:])
                    chunk_refs[k][lines, :] = value.astype(chunk_refs[k].dtype)

        vmem = pl.BlockSpec(memory_space=pltpu.VMEM)
        smem = pl.BlockSpec(memory_space=pltpu.SMEM)
        wide = (2 * rows, 2 * WIDTH)
        dense_outs = [(wide, F32)] + [(wide, BF16)] * 3 + [((width, 8 * rows), BF16)] * 2
        dense_outs = dense_outs + [((896, 2 * WIDTH), BF16)]
        *dense, flat_xt, flat_ct, weights = pl.pallas_call(
            dense_body,
            out_shape=[jax.ShapeDtypeStruct(shape, dtype) for shape, dtype in dense_outs],
            in_specs=[smem] * 2 + [vmem] * 4,
            out_specs=[vmem] * 7,
            cost_estimate=pl.CostEstimate(flops=0, bytes_accessed=0, transcendentals=0),
            compiler_params=pltpu.CompilerParams(vmem_limit_bytes=40 * 1024 * 1024),
        )(my_y.reshape(1), (my_zl % 2).reshape(1), gathered, crossed, two, near)
        dense_in = spread(dense)

    with jax.named_scope("expert_pre"):
        pre_full = kernel(
            lambda a, b: [a + b.astype(F32)], [((48, up.shape[1]), F32)], pre_mine, after(pre_other, *dense)
        )[0]

    with jax.named_scope("expert_hid"):
        hid_mine, hid_other = sum_parts(hid[0], after(hid_in, pre_full))

    with jax.named_scope("dense_dpre"):
        dense_mine, dense_other = sum_parts(dense[0], after(dense_in, hid_mine))

    with jax.named_scope("expert_dpre"):
        dpre = kernel(
            lambda h, o, p: [(h + o.astype(F32)) * silu_slope(p)],
            [((48, up.shape[1]), BF16)],
            hid_mine, after(hid_other, dense_mine), pre_full,
        )[0]
        dpre_other = send(dpre, "zh", 2, 1)

    with jax.named_scope("dense_dpre"):
        total = dense_mine + after(dense_other, dpre).astype(F32)
        d_pre, d_hid = total[:, :WIDTH], total[:, WIDTH:]
        both = jnp.concatenate(
            [(d_hid * silu_slope(d_pre)).astype(BF16), jax.nn.silu(d_pre).astype(BF16)], axis=1
        )
        both_other = send(both, "zh", 2, 1)

    with jax.named_scope("expert_dpre"):
        dpre = both_halves(dpre, after(dpre_other, both), 0)
        dpre_in = [send(dpre, "y", 4, -k) for k in (1, 2, 3)]

    with jax.named_scope("dense_dpre"):
        both = both_halves(both, after(both_other, dpre), 0)
        both_in = [send(both, "y", 4, -k) for k in (1, 2, 3)]

    with jax.named_scope("expert_back"):
        dpre_in = after(dpre_in, both)
        back = dot(jnp.concatenate([dpre] + dpre_in, axis=0), up, 1, 1).astype(BF16).reshape(4, 96, width)
        back = jnp.concatenate([back, back[:3]], axis=0)
        back = lax.dynamic_slice_in_dim(back, (4 - my_y) % 4, 4, 0).reshape(16, 24, width)
        returned = lax.all_to_all(back, ("x", "zl"), split_axis=0, concat_axis=0, tiled=True)
        returned = returned.reshape(384, width)

    with jax.named_scope("dense_grads"):
        whole = jnp.concatenate([both] + after(both_in, back), axis=0)
        lane = jnp.arange(2 * WIDTH) < WIDTH

        def grads_body(odd_ref, xt_ref, ct_ref, whole_ref, keep_ref, give_ref):
            w = whole_ref[...]
            is_up = lax.broadcasted_iota(jnp.int32, (224, 2 * WIDTH), 1) < WIDTH
            for upper in range(2):
                for ref, parity in ((give_ref, 1 - odd_ref[0]), (keep_ref, odd_ref[0])):
                    a = 2 * upper + parity
                    value = jnp.where(is_up, dot(xt_ref[a], w, 1, 0), dot(ct_ref[a], w, 1, 0))
                    ref[upper] = (value * grad_scale).astype(ref.dtype)

        keep, give = pl.pallas_call(
            grads_body,
            out_shape=[jax.ShapeDtypeStruct((2, 224, 2 * WIDTH), t) for t in (F32, BF16)],
            in_specs=[smem] + [vmem] * 3,
            out_specs=[vmem] * 2,
            cost_estimate=pl.CostEstimate(flops=0, bytes_accessed=0, transcendentals=0),
            compiler_params=pltpu.CompilerParams(vmem_limit_bytes=40 * 1024 * 1024),
        )((my_zl % 2).reshape(1), flat_xt.reshape(4, 224, 8 * rows), flat_ct.reshape(4, 224, 8 * rows), whole)
        near_in = swap(give, "zl", 4, 1)

    with jax.named_scope("dense_input"):
        only_dpre = jnp.where(lane[None, :], after(whole, give), 0)
        d_back = dot(only_dpre, weights, 1, 1).reshape(4, 2 * rows, width)
        d_back = jnp.concatenate([d_back, d_back], axis=0)
        d_back = lax.dynamic_slice_in_dim(d_back, (4 - my_y) % 4, 4, 0).reshape(2, 4, rows, width)
        d_cross = send(d_back[1].astype(BF16), "dp", 2, 1)

    with jax.named_scope("expert_combine"):
        info = jnp.concatenate([row_of.astype(F32), ids.reshape(2, rows).astype(F32), gate_values.T], axis=0)
        other_info = send(info, "dp", 2, 1)
        returned = after(returned, d_back)

        def combine(table, target_dp):
            total = jnp.zeros((rows, width), F32)
            for k in (0, 1):
                row = table[k].astype(jnp.int32)
                expert = table[2 + k].astype(jnp.int32)
                row = (expert % 16) * 24 + target_dp * CAP + (row % CAP)
                row = jnp.where(expert // 16 == my_dp, row, -1)
                pick = (row[:, None] == jnp.arange(384, dtype=jnp.int32)[None, :]).astype(BF16)
                total = total + dot(pick, returned, 1, 0) * table[4 + k][:, None]
            return total

        other_input = combine(other_info, 1 - my_dp).astype(BF16)
        other_in = send(other_input, "dp", 2, 1)
        expert_input = combine(info, my_dp)

    with jax.named_scope("dense_grads"):
        keep = (keep + after(near_in, other_input).astype(F32)).astype(BF16)
        upper = my_zl // 2
        mine = lax.dynamic_index_in_dim(keep, upper, 0, keepdims=False)
        give = lax.dynamic_index_in_dim(keep, 1 - upper, 0, keepdims=False)
        total = [
            lax.ppermute(give, AXES, [(b, a) for a, b in weight_moves(2)]),
            lax.ppermute(mine, AXES, [(b, a) for a, b in weight_moves()]),
        ]

    with jax.named_scope("dense_input"):
        d_mine = d_back[0] + after(d_cross, keep).astype(F32)
        my_x = lax.axis_index("x")

        def x_block(k):
            return lax.dynamic_index_in_dim(d_mine, (my_x + k) % 4, 0, keepdims=False)

        d_in = [send(x_block(k).astype(BF16), "x", 4, k) for k in (2, 1, 3)]

    with jax.named_scope("dense_grads"):
        total = (total[0].astype(F32) + total[1].astype(F32)).astype(BF16)
        up_grad = total[:, :WIDTH]
        down_grad = total[:, WIDTH:].T

    with jax.named_scope("input_sum"):
        expert_input = expert_input + other_in.astype(F32)
        dense_input = add_up(x_block(0), after(d_in, total))
        input_grad = (cotangent.astype(F32) + dense_input + expert_input).astype(BF16)
    return (input_grad, up_grad, down_grad)


def solution(mesh):
    split = Mesh(mesh.devices.reshape(SIZES), AXES)
    group, tensor = ("dp", "x", "zl"), ("y", "zh")
    return jax.shard_map(
        local,
        mesh=split,
        in_specs=(
            P(group, tensor),
            P(group, tensor),
            P(group, None),
            P(group, None),
            P(group, tensor),
            P(tensor, group),
            P(group, tensor, None),
            P(group, None, tensor),
        ),
        out_specs=(
            P(group, tensor),
            P(group, tensor),
            P(tensor, group),
        ),
        check_vma=False,
    )
```

```python
import math

import jax
import jax.numpy as jnp
import numpy as np
from jax import lax
from jax.experimental import pallas as pl
from jax.experimental.pallas import tpu as pltpu
from jax.sharding import Mesh, PartitionSpec as P

AXES = ("dp", "x", "zl", "y", "zh")
SIZES = (2, 4, 4, 4, 2)
BF16 = jnp.bfloat16
F32 = jnp.float32
CAP = 12
WIDTH = 304


def weight_moves(flip=0):
    moves = []
    for source in range(256):
        dp, x, zl, y, zh = np.unravel_index(source, SIZES)
        feature_block = dp * 4 + x
        target = np.ravel_multi_index((zh, y, zl ^ flip, feature_block // 2, feature_block % 2), SIZES)
        moves.append((source, int(target)))
    return moves


def silu_slope(values):
    sigma = jax.nn.sigmoid(values)
    return sigma * (1.0 + values * (1.0 - sigma))


def send(values, axis, size, step):
    return lax.ppermute(values, axis, [(i, (i + step) % size) for i in range(size)])


def dot(a, b, ca, cb):
    return lax.dot_general(a, b, (((ca,), (cb,)), ((), ())), preferred_element_type=F32)


def swap(values, axis, size, bit):
    return lax.ppermute(values, axis, [(i, i ^ bit) for i in range(size)])


def kernel(fn, outs, *arrays):
    def body(*refs):
        results = fn(*[r[...] for r in refs[: len(arrays)]])
        for ref, value in zip(refs[len(arrays) :], results, strict=True):
            ref[...] = value.astype(ref.dtype)

    vmem = pl.BlockSpec(memory_space=pltpu.VMEM)
    return pl.pallas_call(
        body,
        out_shape=[jax.ShapeDtypeStruct(shape, dtype) for shape, dtype in outs],
        in_specs=[vmem] * len(arrays),
        out_specs=[vmem] * len(outs),
        cost_estimate=pl.CostEstimate(flops=0, bytes_accessed=0, transcendentals=0),
        compiler_params=pltpu.CompilerParams(vmem_limit_bytes=40 * 1024 * 1024),
    )(*arrays)


def after(values, *earlier):
    return lax.optimization_barrier((values,) + earlier)[0]


def spread(chunks):
    return [send(chunks[k].astype(BF16), "y", 4, k) for k in (2, 1, 3)]


def add_up(own, arriving):
    return own + sum(v.astype(F32) for v in arriving)


def spread_gather(block, axis):
    return jnp.concatenate([block] + [send(block, "y", 4, -k) for k in (1, 2, 3)], axis=axis)


def local(tokens, cotangent, expert_ids, gate_values, dense_up, dense_down, expert_up, expert_down):
    rows = tokens.shape[0]
    width = tokens.shape[1]
    my_dp = lax.axis_index("dp")
    my_y = lax.axis_index("y")
    my_zh = lax.axis_index("zh")
    my_zl = lax.axis_index("zl")
    grad_scale = 1.0 / math.sqrt(rows * 32)
    up = expert_up[0]
    down = expert_down[0]

    with jax.named_scope("route"):
        ids = expert_ids.T.reshape(-1)
        hot = (ids[:, None] == jnp.arange(32, dtype=jnp.int32)[None, :]).astype(F32)
        order = jnp.arange(2 * rows)
        lower = (order[:, None] > order[None, :]).astype(F32)
        before = dot(lower, hot, 1, 0)
        position = jnp.sum(before * hot, axis=1).astype(jnp.int32)
        row_of = ((ids % 16) * 24 + (ids // 16) * CAP + position).reshape(2, rows)
        out_row = jnp.arange(384, dtype=jnp.int32)
        select = (out_row[:, None] == row_of[0][None, :]) | (out_row[:, None] == row_of[1][None, :])
        select = select.astype(BF16)
        packed_x = dot(select, tokens, 1, 0).astype(BF16).reshape(16, 24, width)
        packed_c = dot(select, cotangent, 1, 0).astype(BF16).reshape(16, 24, width)

    with jax.named_scope("to_experts"):
        r = jnp.arange(192, dtype=jnp.int32)
        theirs = (r // CAP) * 24 + (1 - my_dp) * CAP + r % CAP
        rolled = (out_row + my_y * 96) % 384
        block, core, slot = rolled // 24, (rolled // CAP) % 2, rolled % CAP
        from_got = jnp.where(core == my_dp, block * 24 + my_dp * CAP + slot, -1)
        from_other = jnp.where(core == my_dp, -1, block * CAP + slot)
        pick_theirs = (theirs[:, None] == out_row[None, :]).astype(BF16)
        pick_got = (from_got[:, None] == out_row[None, :]).astype(BF16)
        pick_other = (from_other[:, None] == r[None, :]).astype(BF16)

        def to_chip(packed):
            return lax.all_to_all(packed, ("x", "zl"), split_axis=0, concat_axis=0, tiled=True).reshape(384, width)

        def to_core(got):
            theirs = kernel(lambda p, g: [dot(p, g, 1, 0)], [((192, width), BF16)], pick_theirs, got)[0]
            other = send(theirs, "dp", 2, 1)
            return kernel(
                lambda p, g, q, o: [dot(p, g, 1, 0) + dot(q, o, 1, 0)],
                [((384, width), BF16)],
                pick_got, got, pick_other, other,
            )[0]

        got_x = to_chip(packed_x)
        weights = jnp.concatenate([dense_up, dense_down.T], axis=1)
        weights = lax.ppermute(weights, AXES, weight_moves())
        got_c = to_chip(after(packed_c, got_x))
        far = swap(weights, "zl", 4, 2)
        expert_x = to_core(got_x)

    def zh_parts(total, size, axis):
        mine = lax.dynamic_slice_in_dim(total, my_zh * size, size, axis)
        other = lax.dynamic_slice_in_dim(total, (1 - my_zh) * size, size, axis)
        return mine, send(other.astype(BF16), "zh", 2, 1)

    zh_here = jnp.full((8, 128), my_zh, jnp.int32)

    def sum_parts(own, arriving):
        half = (own.shape[0] // 2, own.shape[1])

        def body(own, a, b, c, here):
            total = own + a.astype(F32) + b.astype(F32) + c.astype(F32)
            low, high = total[: half[0]], total[half[0] :]
            first = here[0, 0] == 0
            return jnp.where(first, low, high), jnp.where(first, high, low)

        mine, other = kernel(body, [(half, F32), (half, BF16)], own, *arriving, zh_here)
        return mine, send(other, "zh", 2, 1)

    def both_halves(mine, other, axis):
        return jnp.where(
            my_zh == 0, jnp.concatenate([mine, other], axis), jnp.concatenate([other, mine], axis)
        )

    with jax.named_scope("expert_pre"):
        chunk = (96, up.shape[1])
        chunk_outs = [(chunk, F32)] + [(chunk, BF16)] * 3

        def products(weight_dim):
            def body(lines, weight):
                return [dot(lines[96 * k : 96 * k + 96], weight, 1, weight_dim) for k in range(4)]

            return body

        pre = dict(enumerate(kernel(products(0), chunk_outs, expert_x, up)))
        pre_in = spread(pre)

    with jax.named_scope("tokens_move"):
        gathered = lax.all_gather(jnp.concatenate([tokens, cotangent], axis=0), "x", axis=0)

    with jax.named_scope("expert_hid"):
        expert_c = to_core(after(got_c, weights, *pre.values()))
        hid = dict(enumerate(kernel(products(1), chunk_outs, expert_c, down)))
        hid_in = spread(hid)

    with jax.named_scope("expert_pre"):
        pre_in, gathered, far = after([pre_in, gathered, far], *hid.values())
        low = my_zl < 2
        two = jnp.stack([jnp.where(low, weights, far), jnp.where(low, far, weights)])
        near = swap(two, "zl", 4, 1)
        pre_mine, pre_other = sum_parts(pre[0], pre_in)

    with jax.named_scope("tokens_move"):
        crossed = send(gathered, "dp", 2, 1)

    with jax.named_scope("dense_sums"):
        def dense_body(y_ref, even_ref, own_ref, cross_ref, two_ref, near_ref, *outs):
            chunk_refs, xt_ref, ct_ref, w_ref = outs[:4], outs[4], outs[5], outs[6]
            even = even_ref[0] == 0
            for upper in range(2):
                a, b = two_ref[upper], near_ref[upper]
                w_ref[448 * upper : 448 * upper + 224, :] = jnp.where(even, a, b)
                w_ref[448 * upper + 224 : 448 * upper + 448, :] = jnp.where(even, b, a)
            is_pre = lax.broadcasted_iota(jnp.int32, (rows, 2 * WIDTH), 1) < WIDTH
            for k in range(4):
                block = lax.rem(y_ref[0] + k, 4)
                first = 2 * lax.rem(block, 2)
                w = w_ref[...]
                for i in range(2):
                    both = jnp.where(block < 2, own_ref[first + i], cross_ref[first + i])
                    lines = pl.ds(rows * i, rows)
                    lanes = pl.ds(2 * rows * k + rows * i, rows)
                    xt_ref[:, lanes] = both[:rows].T
                    ct_ref[:, lanes] = both[rows:].T
                    products = dot(both, w, 1, 0)
                    value = jnp.where(is_pre, products[:rows], products[rows:])
                    chunk_refs[k][lines, :] = value.astype(chunk_refs[k].dtype)

        vmem = pl.BlockSpec(memory_space=pltpu.VMEM)
        smem = pl.BlockSpec(memory_space=pltpu.SMEM)
        wide = (2 * rows, 2 * WIDTH)
        dense_outs = [(wide, F32)] + [(wide, BF16)] * 3 + [((width, 8 * rows), BF16)] * 2
        dense_outs = dense_outs + [((896, 2 * WIDTH), BF16)]
        *dense, flat_xt, flat_ct, weights = pl.pallas_call(
            dense_body,
            out_shape=[jax.ShapeDtypeStruct(shape, dtype) for shape, dtype in dense_outs],
            in_specs=[smem] * 2 + [vmem] * 4,
            out_specs=[vmem] * 7,
            cost_estimate=pl.CostEstimate(flops=0, bytes_accessed=0, transcendentals=0),
            compiler_params=pltpu.CompilerParams(vmem_limit_bytes=40 * 1024 * 1024),
        )(my_y.reshape(1), (my_zl % 2).reshape(1), gathered, crossed, two, near)
        dense_in = spread(dense)

    with jax.named_scope("expert_pre"):
        pre_full = kernel(
            lambda a, b: [a + b.astype(F32)], [((48, up.shape[1]), F32)], pre_mine, after(pre_other, *dense)
        )[0]

    with jax.named_scope("expert_hid"):
        hid_mine, hid_other = sum_parts(hid[0], after(hid_in, pre_full))

    with jax.named_scope("expert_dpre"):
        dpre = kernel(
            lambda h, o, p: [(h + o.astype(F32)) * silu_slope(p)],
            [((48, up.shape[1]), BF16)],
            hid_mine, hid_other, pre_full,
        )[0]
        dpre_other = send(dpre, "zh", 2, 1)

    with jax.named_scope("dense_dpre"):
        dense_mine, dense_other = sum_parts(dense[0], after(dense_in, dpre))

    with jax.named_scope("expert_dpre"):
        dpre_full = both_halves(dpre, after(dpre_other, dense_mine), 0)

    with jax.named_scope("dense_dpre"):
        total = dense_mine + after(dense_other, dpre_full).astype(F32)
        d_pre, d_hid = total[:, :WIDTH], total[:, WIDTH:]
        both = jnp.concatenate(
            [(d_hid * silu_slope(d_pre)).astype(BF16), jax.nn.silu(d_pre).astype(BF16)], axis=1
        )
        both_other = send(both, "zh", 2, 1)

    with jax.named_scope("expert_dpre"):
        dpre_in = [send(dpre_full, "y", 4, -k) for k in (1, 2, 3)]

    with jax.named_scope("dense_dpre"):
        both = both_halves(both, both_other, 0)
        both_in = [send(both, "y", 4, -k) for k in (1, 2, 3)]

    with jax.named_scope("expert_back"):
        dpre_in = after(dpre_in, both)
        back = dot(jnp.concatenate([dpre_full] + dpre_in, axis=0), up, 1, 1).astype(BF16).reshape(4, 96, width)
        back = jnp.concatenate([back, back[:3]], axis=0)
        back = lax.dynamic_slice_in_dim(back, (4 - my_y) % 4, 4, 0).reshape(16, 24, width)
        returned = lax.all_to_all(back, ("x", "zl"), split_axis=0, concat_axis=0, tiled=True)
        returned = returned.reshape(384, width)

    with jax.named_scope("dense_grads"):
        whole = jnp.concatenate([both] + after(both_in, back), axis=0)
        lane = jnp.arange(2 * WIDTH) < WIDTH

        def grads_body(odd_ref, xt_ref, ct_ref, whole_ref, keep_ref, give_ref):
            w = whole_ref[...]
            is_up = lax.broadcasted_iota(jnp.int32, (224, 2 * WIDTH), 1) < WIDTH
            for upper in range(2):
                for ref, parity in ((give_ref, 1 - odd_ref[0]), (keep_ref, odd_ref[0])):
                    a = 2 * upper + parity
                    value = jnp.where(is_up, dot(xt_ref[a], w, 1, 0), dot(ct_ref[a], w, 1, 0))
                    ref[upper] = (value * grad_scale).astype(ref.dtype)

        keep, give = pl.pallas_call(
            grads_body,
            out_shape=[jax.ShapeDtypeStruct((2, 224, 2 * WIDTH), t) for t in (F32, BF16)],
            in_specs=[smem] + [vmem] * 3,
            out_specs=[vmem] * 2,
            cost_estimate=pl.CostEstimate(flops=0, bytes_accessed=0, transcendentals=0),
            compiler_params=pltpu.CompilerParams(vmem_limit_bytes=40 * 1024 * 1024),
        )((my_zl % 2).reshape(1), flat_xt.reshape(4, 224, 8 * rows), flat_ct.reshape(4, 224, 8 * rows), whole)
        near_in = swap(give, "zl", 4, 1)

    with jax.named_scope("dense_input"):
        only_dpre = jnp.where(lane[None, :], after(whole, give), 0)
        d_back = dot(only_dpre, weights, 1, 1).reshape(4, 2 * rows, width)
        d_back = jnp.concatenate([d_back, d_back], axis=0)
        d_back = lax.dynamic_slice_in_dim(d_back, (4 - my_y) % 4, 4, 0).reshape(2, 4, rows, width)
        d_cross = send(d_back[1].astype(BF16), "dp", 2, 1)

    with jax.named_scope("expert_combine"):
        info = jnp.concatenate([row_of.astype(F32), ids.reshape(2, rows).astype(F32), gate_values.T], axis=0)
        other_info = send(info, "dp", 2, 1)
        returned = after(returned, d_back)

        def combine(table, target_dp):
            total = jnp.zeros((rows, width), F32)
            for k in (0, 1):
                row = table[k].astype(jnp.int32)
                expert = table[2 + k].astype(jnp.int32)
                row = (expert % 16) * 24 + target_dp * CAP + (row % CAP)
                row = jnp.where(expert // 16 == my_dp, row, -1)
                pick = (row[:, None] == jnp.arange(384, dtype=jnp.int32)[None, :]).astype(BF16)
                total = total + dot(pick, returned, 1, 0) * table[4 + k][:, None]
            return total

        other_input = combine(other_info, 1 - my_dp).astype(BF16)
        other_in = send(other_input, "dp", 2, 1)
        expert_input = combine(info, my_dp)

    with jax.named_scope("dense_grads"):
        keep = keep + after(near_in, other_input).astype(F32)
        upper = my_zl // 2
        mine = lax.dynamic_index_in_dim(keep, upper, 0, keepdims=False)
        give = lax.dynamic_index_in_dim(keep, 1 - upper, 0, keepdims=False).astype(BF16)
        far_in = swap(give, "zl", 4, 2)

    with jax.named_scope("dense_input"):
        d_mine = d_back[0] + after(d_cross, keep).astype(F32)
        my_x = lax.axis_index("x")

        def x_block(k):
            return lax.dynamic_index_in_dim(d_mine, (my_x + k) % 4, 0, keepdims=False)

        d_in = [send(x_block(k).astype(BF16), "x", 4, k) for k in (2, 1, 3)]

    with jax.named_scope("dense_grads"):
        total = (mine + after(far_in, d_mine).astype(F32)).astype(BF16)
        total = lax.ppermute(total, AXES, [(b, a) for a, b in weight_moves()])
        up_grad = total[:, :WIDTH]
        down_grad = total[:, WIDTH:].T

    with jax.named_scope("input_sum"):
        expert_input = expert_input + other_in.astype(F32)
        dense_input = add_up(x_block(0), after(d_in, total))
        input_grad = (cotangent.astype(F32) + dense_input + expert_input).astype(BF16)
    return (input_grad, up_grad, down_grad)


def solution(mesh):
    split = Mesh(mesh.devices.reshape(SIZES), AXES)
    group, tensor = ("dp", "x", "zl"), ("y", "zh")
    return jax.shard_map(
        local,
        mesh=split,
        in_specs=(
            P(group, tensor),
            P(group, tensor),
            P(group, None),
            P(group, None),
            P(group, tensor),
            P(tensor, group),
            P(group, tensor, None),
            P(group, None, tensor),
        ),
        out_specs=(
            P(group, tensor),
            P(group, tensor),
            P(tensor, group),
        ),
        check_vma=False,
    )
```

```python
import math

import jax
import jax.numpy as jnp
import numpy as np
from jax import lax
from jax.experimental import pallas as pl
from jax.experimental.pallas import tpu as pltpu
from jax.sharding import Mesh, PartitionSpec as P

AXES = ("dp", "x", "zl", "y", "zh")
SIZES = (2, 4, 4, 4, 2)
BF16 = jnp.bfloat16
F32 = jnp.float32
CAP = 12
WIDTH = 304


def weight_moves(flip=0):
    moves = []
    for source in range(256):
        dp, x, zl, y, zh = np.unravel_index(source, SIZES)
        feature_block = dp * 4 + x
        target = np.ravel_multi_index((zh, y, zl ^ flip, feature_block // 2, feature_block % 2), SIZES)
        moves.append((source, int(target)))
    return moves


def silu_slope(values):
    sigma = jax.nn.sigmoid(values)
    return sigma * (1.0 + values * (1.0 - sigma))


def send(values, axis, size, step):
    return lax.ppermute(values, axis, [(i, (i + step) % size) for i in range(size)])


def dot(a, b, ca, cb):
    return lax.dot_general(a, b, (((ca,), (cb,)), ((), ())), preferred_element_type=F32)


def swap(values, axis, size, bit):
    return lax.ppermute(values, axis, [(i, i ^ bit) for i in range(size)])


def kernel(fn, outs, *arrays):
    def body(*refs):
        results = fn(*[r[...] for r in refs[: len(arrays)]])
        for ref, value in zip(refs[len(arrays) :], results, strict=True):
            ref[...] = value.astype(ref.dtype)

    vmem = pl.BlockSpec(memory_space=pltpu.VMEM)
    return pl.pallas_call(
        body,
        out_shape=[jax.ShapeDtypeStruct(shape, dtype) for shape, dtype in outs],
        in_specs=[vmem] * len(arrays),
        out_specs=[vmem] * len(outs),
        cost_estimate=pl.CostEstimate(flops=0, bytes_accessed=0, transcendentals=0),
        compiler_params=pltpu.CompilerParams(vmem_limit_bytes=40 * 1024 * 1024),
    )(*arrays)


def after(values, *earlier):
    return lax.optimization_barrier((values,) + earlier)[0]


def spread(chunks):
    return [send(chunks[k].astype(BF16), "y", 4, k) for k in (2, 1, 3)]


def add_up(own, arriving):
    return own + sum(v.astype(F32) for v in arriving)


def spread_gather(block, axis):
    return jnp.concatenate([block] + [send(block, "y", 4, -k) for k in (1, 2, 3)], axis=axis)


def local(tokens, cotangent, expert_ids, gate_values, dense_up, dense_down, expert_up, expert_down):
    rows = tokens.shape[0]
    width = tokens.shape[1]
    my_dp = lax.axis_index("dp")
    my_y = lax.axis_index("y")
    my_zh = lax.axis_index("zh")
    my_zl = lax.axis_index("zl")
    grad_scale = 1.0 / math.sqrt(rows * 32)
    up = expert_up[0]
    down = expert_down[0]

    with jax.named_scope("route"):
        ids = expert_ids.T.reshape(-1)
        hot = (ids[:, None] == jnp.arange(32, dtype=jnp.int32)[None, :]).astype(F32)
        order = jnp.arange(2 * rows)
        lower = (order[:, None] > order[None, :]).astype(F32)
        before = dot(lower, hot, 1, 0)
        position = jnp.sum(before * hot, axis=1).astype(jnp.int32)
        row_of = ((ids % 16) * 24 + (ids // 16) * CAP + position).reshape(2, rows)
        out_row = jnp.arange(384, dtype=jnp.int32)
        select = (out_row[:, None] == row_of[0][None, :]) | (out_row[:, None] == row_of[1][None, :])
        select = select.astype(BF16)
        packed_x = dot(select, tokens, 1, 0).astype(BF16).reshape(16, 24, width)
        packed_c = dot(select, cotangent, 1, 0).astype(BF16).reshape(16, 24, width)

    with jax.named_scope("to_experts"):
        r = jnp.arange(192, dtype=jnp.int32)
        theirs = (r // CAP) * 24 + (1 - my_dp) * CAP + r % CAP
        rolled = (out_row + my_y * 96) % 384
        block, core, slot = rolled // 24, (rolled // CAP) % 2, rolled % CAP
        from_got = jnp.where(core == my_dp, block * 24 + my_dp * CAP + slot, -1)
        from_other = jnp.where(core == my_dp, -1, block * CAP + slot)
        pick_theirs = (theirs[:, None] == out_row[None, :]).astype(BF16)
        pick_got = (from_got[:, None] == out_row[None, :]).astype(BF16)
        pick_other = (from_other[:, None] == r[None, :]).astype(BF16)

        def to_chip(packed):
            return lax.all_to_all(packed, ("x", "zl"), split_axis=0, concat_axis=0, tiled=True).reshape(384, width)

        def to_core(got):
            theirs = kernel(lambda p, g: [dot(p, g, 1, 0)], [((192, width), BF16)], pick_theirs, got)[0]
            other = send(theirs, "dp", 2, 1)
            return kernel(
                lambda p, g, q, o: [dot(p, g, 1, 0) + dot(q, o, 1, 0)],
                [((384, width), BF16)],
                pick_got, got, pick_other, other,
            )[0]

        got_x = to_chip(packed_x)
        weights = jnp.concatenate([dense_up, dense_down.T], axis=1)
        weights = lax.ppermute(weights, AXES, weight_moves())
        got_c = to_chip(after(packed_c, got_x))
        far = swap(weights, "zl", 4, 2)
        expert_x = to_core(got_x)

    def zh_parts(total, size, axis):
        mine = lax.dynamic_slice_in_dim(total, my_zh * size, size, axis)
        other = lax.dynamic_slice_in_dim(total, (1 - my_zh) * size, size, axis)
        return mine, send(other.astype(BF16), "zh", 2, 1)

    zh_here = jnp.full((8, 128), my_zh, jnp.int32)

    def sum_parts(own, arriving):
        half = (own.shape[0] // 2, own.shape[1])

        def body(own, a, b, c, here):
            total = own + a.astype(F32) + b.astype(F32) + c.astype(F32)
            low, high = total[: half[0]], total[half[0] :]
            first = here[0, 0] == 0
            return jnp.where(first, low, high), jnp.where(first, high, low)

        mine, other = kernel(body, [(half, F32), (half, BF16)], own, *arriving, zh_here)
        return mine, send(other, "zh", 2, 1)

    def both_halves(mine, other, axis):
        return jnp.where(
            my_zh == 0, jnp.concatenate([mine, other], axis), jnp.concatenate([other, mine], axis)
        )

    with jax.named_scope("expert_pre"):
        chunk = (96, up.shape[1])
        chunk_outs = [(chunk, F32)] + [(chunk, BF16)] * 3

        def products(weight_dim):
            def body(lines, weight):
                return [dot(lines[96 * k : 96 * k + 96], weight, 1, weight_dim) for k in range(4)]

            return body

        pre = dict(enumerate(kernel(products(0), chunk_outs, expert_x, up)))
        pre_in = spread(pre)

    with jax.named_scope("tokens_move"):
        gathered = lax.all_gather(jnp.concatenate([tokens, cotangent], axis=0), "x", axis=0)

    with jax.named_scope("expert_hid"):
        expert_c = to_core(after(got_c, weights, *pre.values()))
        hid = dict(enumerate(kernel(products(1), chunk_outs, expert_c, down)))
        hid_in = spread(hid)

    with jax.named_scope("expert_pre"):
        pre_in, gathered, far = after([pre_in, gathered, far], *hid.values())
        low = my_zl < 2
        two = jnp.stack([jnp.where(low, weights, far), jnp.where(low, far, weights)])
        near = swap(two, "zl", 4, 1)
        pre_mine, pre_other = sum_parts(pre[0], pre_in)

    with jax.named_scope("tokens_move"):
        crossed = send(gathered, "dp", 2, 1)

    with jax.named_scope("dense_sums"):
        def dense_body(y_ref, even_ref, own_ref, cross_ref, two_ref, near_ref, *outs):
            chunk_refs, xt_ref, ct_ref, w_ref = outs[:4], outs[4], outs[5], outs[6]
            even = even_ref[0] == 0
            for upper in range(2):
                a, b = two_ref[upper], near_ref[upper]
                w_ref[448 * upper : 448 * upper + 224, :] = jnp.where(even, a, b)
                w_ref[448 * upper + 224 : 448 * upper + 448, :] = jnp.where(even, b, a)
            is_pre = lax.broadcasted_iota(jnp.int32, (rows, 2 * WIDTH), 1) < WIDTH
            for k in range(4):
                block = lax.rem(y_ref[0] + k, 4)
                first = 2 * lax.rem(block, 2)
                w = w_ref[...]
                for i in range(2):
                    both = jnp.where(block < 2, own_ref[first + i], cross_ref[first + i])
                    lines = pl.ds(rows * i, rows)
                    lanes = pl.ds(2 * rows * k + rows * i, rows)
                    xt_ref[:, lanes] = both[:rows].T
                    ct_ref[:, lanes] = both[rows:].T
                    products = dot(both, w, 1, 0)
                    value = jnp.where(is_pre, products[:rows], products[rows:])
                    chunk_refs[k][lines, :] = value.astype(chunk_refs[k].dtype)

        vmem = pl.BlockSpec(memory_space=pltpu.VMEM)
        smem = pl.BlockSpec(memory_space=pltpu.SMEM)
        wide = (2 * rows, 2 * WIDTH)
        dense_outs = [(wide, F32)] + [(wide, BF16)] * 3 + [((width, 8 * rows), BF16)] * 2
        dense_outs = dense_outs + [((896, 2 * WIDTH), BF16)]
        *dense, flat_xt, flat_ct, weights = pl.pallas_call(
            dense_body,
            out_shape=[jax.ShapeDtypeStruct(shape, dtype) for shape, dtype in dense_outs],
            in_specs=[smem] * 2 + [vmem] * 4,
            out_specs=[vmem] * 7,
            cost_estimate=pl.CostEstimate(flops=0, bytes_accessed=0, transcendentals=0),
            compiler_params=pltpu.CompilerParams(vmem_limit_bytes=40 * 1024 * 1024),
        )(my_y.reshape(1), (my_zl % 2).reshape(1), gathered, crossed, two, near)
        dense_in = spread(dense)

    with jax.named_scope("expert_pre"):
        pre_full = kernel(
            lambda a, b: [a + b.astype(F32)], [((48, up.shape[1]), F32)], pre_mine, after(pre_other, *dense)
        )[0]

    with jax.named_scope("expert_hid"):
        hid_mine, hid_other = sum_parts(hid[0], after(hid_in, pre_full))

    with jax.named_scope("expert_dpre"):
        dpre = kernel(
            lambda h, o, p: [(h + o.astype(F32)) * silu_slope(p)],
            [((48, up.shape[1]), BF16)],
            hid_mine, hid_other, pre_full,
        )[0]
        dpre_other = send(dpre, "zh", 2, 1)

    with jax.named_scope("dense_dpre"):
        dense_mine, dense_other = sum_parts(dense[0], after(dense_in, dpre))

    with jax.named_scope("expert_dpre"):
        dpre_full = both_halves(dpre, after(dpre_other, dense_mine), 0)

    with jax.named_scope("dense_dpre"):
        total = dense_mine + after(dense_other, dpre_full).astype(F32)
        d_pre, d_hid = total[:, :WIDTH], total[:, WIDTH:]
        both = jnp.concatenate(
            [(d_hid * silu_slope(d_pre)).astype(BF16), jax.nn.silu(d_pre).astype(BF16)], axis=1
        )
        both_other = send(both, "zh", 2, 1)

    with jax.named_scope("expert_dpre"):
        dpre_in = [send(dpre_full, "y", 4, -k) for k in (1, 2, 3)]

    with jax.named_scope("dense_dpre"):
        both = both_halves(both, both_other, 0)
        both_in = [send(both, "y", 4, -k) for k in (1, 2, 3)]

    with jax.named_scope("expert_back"):
        dpre_in = after(dpre_in, both)
        back = dot(jnp.concatenate([dpre_full] + dpre_in, axis=0), up, 1, 1).astype(BF16).reshape(4, 96, width)
        back = jnp.concatenate([back, back[:3]], axis=0)
        back = lax.dynamic_slice_in_dim(back, (4 - my_y) % 4, 4, 0).reshape(16, 24, width)
        returned = lax.all_to_all(back, ("x", "zl"), split_axis=0, concat_axis=0, tiled=True)
        returned = returned.reshape(384, width)

    with jax.named_scope("dense_grads"):
        whole = jnp.concatenate([both] + after(both_in, back), axis=0)
        lane = jnp.arange(2 * WIDTH) < WIDTH

        def grads_body(odd_ref, xt_ref, ct_ref, whole_ref, keep_ref, give_ref):
            w = whole_ref[...]
            is_up = lax.broadcasted_iota(jnp.int32, (224, 2 * WIDTH), 1) < WIDTH
            for upper in range(2):
                for ref, parity in ((give_ref, 1 - odd_ref[0]), (keep_ref, odd_ref[0])):
                    a = 2 * upper + parity
                    value = jnp.where(is_up, dot(xt_ref[a], w, 1, 0), dot(ct_ref[a], w, 1, 0))
                    ref[upper] = (value * grad_scale).astype(ref.dtype)

        keep, give = pl.pallas_call(
            grads_body,
            out_shape=[jax.ShapeDtypeStruct((2, 224, 2 * WIDTH), t) for t in (F32, BF16)],
            in_specs=[smem] + [vmem] * 3,
            out_specs=[vmem] * 2,
            cost_estimate=pl.CostEstimate(flops=0, bytes_accessed=0, transcendentals=0),
            compiler_params=pltpu.CompilerParams(vmem_limit_bytes=40 * 1024 * 1024),
        )((my_zl % 2).reshape(1), flat_xt.reshape(4, 224, 8 * rows), flat_ct.reshape(4, 224, 8 * rows), whole)
        near_in = swap(give, "zl", 4, 1)

    with jax.named_scope("dense_input"):
        only_dpre = jnp.where(lane[None, :], after(whole, give), 0)
        d_back = dot(only_dpre, weights, 1, 1).reshape(4, 2 * rows, width)
        d_back = jnp.concatenate([d_back, d_back], axis=0)
        d_back = lax.dynamic_slice_in_dim(d_back, (4 - my_y) % 4, 4, 0).reshape(2, 4, rows, width)
        d_cross = send(d_back[1].astype(BF16), "dp", 2, 1)

    with jax.named_scope("dense_grads"):
        keep = keep + after(near_in, d_back).astype(F32)
        upper = my_zl // 2
        mine = lax.dynamic_index_in_dim(keep, upper, 0, keepdims=False)
        give = lax.dynamic_index_in_dim(keep, 1 - upper, 0, keepdims=False).astype(BF16)
        far_in = swap(give, "zl", 4, 2)

    with jax.named_scope("dense_input"):
        d_mine = d_back[0] + after(d_cross, keep).astype(F32)
        my_x = lax.axis_index("x")

        def x_block(k):
            return lax.dynamic_index_in_dim(d_mine, (my_x + k) % 4, 0, keepdims=False)

        d_in = [send(x_block(k).astype(BF16), "x", 4, k) for k in (2, 1, 3)]

    with jax.named_scope("dense_grads"):
        total = (mine + after(far_in, d_mine).astype(F32)).astype(BF16)

    with jax.named_scope("expert_combine"):
        info = jnp.concatenate([row_of.astype(F32), ids.reshape(2, rows).astype(F32), gate_values.T], axis=0)
        other_info = send(info, "dp", 2, 1)
        returned = after(returned, total)

        def combine(table, target_dp):
            total = jnp.zeros((rows, width), F32)
            for k in (0, 1):
                row = table[k].astype(jnp.int32)
                expert = table[2 + k].astype(jnp.int32)
                row = (expert % 16) * 24 + target_dp * CAP + (row % CAP)
                row = jnp.where(expert // 16 == my_dp, row, -1)
                pick = (row[:, None] == jnp.arange(384, dtype=jnp.int32)[None, :]).astype(BF16)
                total = total + dot(pick, returned, 1, 0) * table[4 + k][:, None]
            return total

        other_input = combine(other_info, 1 - my_dp).astype(BF16)
        other_in = send(other_input, "dp", 2, 1)
        expert_input = combine(info, my_dp)

    with jax.named_scope("dense_grads"):
        total = lax.ppermute(total, AXES, [(b, a) for a, b in weight_moves()])
        up_grad = total[:, :WIDTH]
        down_grad = total[:, WIDTH:].T

    with jax.named_scope("input_sum"):
        expert_input = expert_input + other_in.astype(F32)
        dense_input = add_up(x_block(0), after(d_in, total))
        input_grad = (cotangent.astype(F32) + dense_input + expert_input).astype(BF16)
    return (input_grad, up_grad, down_grad)


def solution(mesh):
    split = Mesh(mesh.devices.reshape(SIZES), AXES)
    group, tensor = ("dp", "x", "zl"), ("y", "zh")
    return jax.shard_map(
        local,
        mesh=split,
        in_specs=(
            P(group, tensor),
            P(group, tensor),
            P(group, None),
            P(group, None),
            P(group, tensor),
            P(tensor, group),
            P(group, tensor, None),
            P(group, None, tensor),
        ),
        out_specs=(
            P(group, tensor),
            P(group, tensor),
            P(tensor, group),
        ),
        check_vma=False,
    )
```
